768 devices in a mesh: gx: 24 (over x, z_lo), gy: 32 (over z_hi, y, core).
Axes of the slice: x: 4, y: 8, z: 12 (z_hi: 2, z_lo: 6; z = z_hi * 6 + z_lo), core: 2. Of those that a mesh axis runs over, the one named last changes fastest.
Arguments:
- inputs: bfloat16 [768, 12288], P('gx', 'gy'), may hold values from -6 to 6
- preact: bfloat16 [768, 24576], P('gy', 'gx'), may hold values from -6 to 6
- w_in: bfloat16 [12288, 24576], P('gy', 'gx'), may hold values from -0.0546875 to 0.0546875
- w_out: bfloat16 [24576, 12288], P('gx', 'gy'), may hold values from -0.0390625 to 0.0390625
- out_grad: bfloat16 [768, 12288], P('gx', 'gy'), may hold values from -6 to 6
Outputs:
- grad_inputs: bfloat16 [768, 12288], P('gx', 'gy')
- grad_w_in: bfloat16 [12288, 24576], P('gy', 'gx')
- grad_w_out: bfloat16 [24576, 12288], P('gx', 'gy')
The draws below stay inside these ranges and needn't reach their ends.
All inputs are finite; a program needn't handle non-finite values.
Results may differ from the reference program's by a relative error of at most 0.0049.
Values may be sent and summed in bfloat16 or wider, within the bound.
A program may use at most 32 MiB of HBM per device.

```python
import jax
import jax.numpy as jnp
from jax import lax

D = 12288
FF = 24576
TOKENS = 768


def spiked(values, stream_key, source, target, blocks, factor):
    owner, partner = [(jnp.arange(values.shape[dim]) // (values.shape[dim] // blocks)).reshape([-1 if axis == dim else 1 for axis in range(values.ndim)]) for dim in (source, target)]
    chosen = jax.random.permutation(stream_key, blocks)[partner]
    strong = (owner == chosen) | (owner == (partner + blocks // 2) % blocks)
    return jnp.where(strong, factor * values, values)


def block_scale(own_key, extent, pieces, low, largest):
    gain, own = 1.0, jax.random.fold_in(own_key, 6)
    for dim, shards_of in pieces:
        heights = jnp.exp(jax.random.uniform(jax.random.fold_in(own, dim), (shards_of,), jnp.float32, low / len(pieces), largest / len(pieces)))
        gain = gain * jnp.repeat(heights, extent[dim] // shards_of).reshape([-1 if axis == dim else 1 for axis in range(len(extent))])
    return gain


def gaussian(own_key, shape, scale, limit, cuts=(), kind=jnp.bfloat16):
    array = scale * jax.random.normal(own_key, shape, jnp.float32)
    if cuts:
        array = array * block_scale(own_key, shape, cuts, -0.22, 0.18)
    return jnp.clip(array, -limit, limit).astype(kind)


def noise_with(stream_key, shape, scale, limit, split, heavy, held_as=jnp.bfloat16):
    result = scale * jax.random.normal(stream_key, shape, jnp.float32)
    if split:
        result = result * block_scale(stream_key, shape, split, -0.22, 0.18)
    return jnp.clip(spiked(result, jax.random.fold_in(stream_key, 3), *heavy), -limit, limit).astype(held_as)


def setup_inputs(seed: int = 0) -> dict:
    seeds = jax.random.split(jax.random.key(seed), 6)
    return {
        "inputs": gaussian(seeds[0], (TOKENS, D), 1.0, 6.0, ((0, 24), (1, 32))),
        "preact": gaussian(seeds[1], (TOKENS, FF), 1.5, 6.0, ((0, 32), (1, 24))),
        "w_in": gaussian(seeds[2], (D, FF), D ** -0.5, 0.0546875, ((0, 32), (1, 24))),
        "w_out": gaussian(seeds[3], (FF, D), FF ** -0.5, 0.0390625, ((0, 24), (1, 32))),
        "out_grad": noise_with(seeds[4], (TOKENS, D), 1.0, 6.0, ((0, 24), (1, 32)), (1, 0, 32, 2.75)),
    }


gelu_scale = 0.7978845608028654
cubic_coef = 0.044715


def activation_pair(grad_act, preact):
    values = preact.astype(jnp.float32)
    argument = gelu_scale * (values + cubic_coef * values * values * values)
    tangent = jnp.tanh(argument)
    acts = (0.5 * values * (1.0 + tangent)).astype(jnp.bfloat16)
    slope = 0.5 * (1.0 + tangent) + 0.5 * values * (1.0 - tangent * tangent) * gelu_scale * (1.0 + 3.0 * cubic_coef * values * values)
    return acts, (grad_act * slope).astype(jnp.bfloat16)


def reference(inputs, preact, w_in, w_out, out_grad):
    grad_act = lax.dot_general(out_grad, w_out, (((1,), (1,)), ((), ())), preferred_element_type=jnp.float32)
    acts, grad_hidden = activation_pair(grad_act, preact)
    grad_w_out = lax.dot_general(acts, out_grad, (((0,), (0,)), ((), ())), preferred_element_type=jnp.float32).astype(jnp.bfloat16)
    grad_w_in = lax.dot_general(inputs, grad_hidden, (((0,), (0,)), ((), ())), preferred_element_type=jnp.float32).astype(jnp.bfloat16)
    grad_inputs = lax.dot_general(grad_hidden, w_in, (((1,), (1,)), ((), ())), preferred_element_type=jnp.float32).astype(jnp.bfloat16)
    return grad_inputs, grad_w_in, grad_w_out
```

```python
import functools

import jax
import jax.numpy as jnp
from jax import lax
from jax.experimental import pallas as pl
from jax.experimental.pallas import tpu as pltpu
from jax.sharding import PartitionSpec as P

gelu_scale = 0.7978845608028654
cubic_coef = 0.044715
MESH = pl.DeviceIdType.MESH
NX = 4
K = 2
bf16, f32 = jnp.bfloat16, jnp.float32


def activation(values):
    argument = gelu_scale * (values + cubic_coef * values * values * values)
    tangent = jnp.tanh(argument)
    acts = (0.5 * values * (1.0 + tangent)).astype(bf16)
    slope = 0.5 * (1.0 + tangent) + 0.5 * values * (1.0 - tangent * tangent) * gelu_scale * (
        1.0 + 3.0 * cubic_coef * values * values
    )
    return acts, slope


def dot_nt(a, b):
    return lax.dot_general(a, b, (((1,), (1,)), ((), ())), preferred_element_type=f32)


def dot_tn(a, b):
    return lax.dot_general(a, b, (((0,), (0,)), ((), ())), preferred_element_type=f32)


class Counter:
    def __init__(self):
        self.n = 0

    def take(self, n=1):
        base = self.n
        self.n += n
        return base


def layout(NZ, NY):
    c, r = Counter(), {}
    for name, n in (
        ("og_z", NZ), ("og_x", 6), ("og_c", 2 * NX), ("in_z", NZ), ("in_x", 6),
        ("wo", 1), ("pre_c", 1), ("pre_z", 1),
        ("act_l", 2 * (NY // 2)), ("act_s", 2 * (NY // 2)), ("act_c", 2 * NY),
        ("rs_l", K * (NY // 2)), ("rs_s", K * (NY // 2)), ("zx", K),
        ("gh_l", K * (NY // 2)), ("gh_s", K * (NY // 2)), ("gh_c", K * NY),
        ("xs", 3 * (2 * NY // NX)), ("zs", NZ),
    ):
        r[name] = c.take(n)
    return r, c.n


def count_sends(NZ, NY):
    return 2 * ((NZ - 1) + 6) + 2 * NX + 3 + 2 * (NY - 1 + NY) + K * (NY - 1) + K + K * (2 * NY - 1) + 2 * NY + NZ - 1


def kernel(
    NZ, NY, in_ref, pre_ref, wi_hbm, wo_hbm, og_ref,
    gi_ref, gwi_hbm, gwo_hbm,
    og, ogo, inp, wi, wo, wo_oth, pre_s, pre_r, prez_s, prez_r, slope, acts, part,
    rl_s, rl_r, rs_s, rs_r, tot, zx_s, zx_r, gh, xs_s, xs_r, xs_own, z_own, z_s, z_r, gwi, gwo,
    send, recv, local,
):
    NZg = NZ // 2
    R, W = og_ref.shape
    H = wo_hbm.shape[0]
    Hh, HC = H // 2, H // 2 // K
    T = R * NX * NZ
    XR = R * NZ
    B = T // (2 * NY)
    TB = B // 2
    LL, LS = NY // 2, NY // 2 - 1
    BX = 2 * NY // NX
    S, _ = layout(NZ, NY)

    gx, gy = lax.axis_index("gx"), lax.axis_index("gy")
    x, zl = gx // NZ, gx % NZ
    zh, y, c = gy // (2 * NY), (gy // 2) % NY, gy % 2
    oc = 1 - c
    sg = 1 - 2 * c

    def dev(x=x, zl=zl, zh=zh, y=y, c=c):
        return (x * NZ + zl, (zh * NY + y) * 2 + c)

    def ym(v):
        return lax.rem(v + 2 * NY, NY)

    def xm(v):
        return lax.rem(v + 2 * NX, NX)

    core, zpar = dev(c=oc), dev(zh=1 - zh)
    xr, xl, xo = dev(x=xm(x + 1)), dev(x=xm(x - 1)), dev(x=xm(x + 2))
    zoff = sorted(range(1, NZ), key=lambda o: min(o, NZ - o))
    zpeer = {o: lax.rem(zl + o, NZ) for o in zoff}

    sends = []

    def rcopy(src, dst, ri, to, when=None):
        cp = pltpu.make_async_remote_copy(src, dst, send.at[len(sends)], recv.at[ri], device_id=to, device_id_type=MESH)
        sends.append((cp, when))
        if when is None:
            cp.start()
        else:
            pl.when(when)(cp.start)

    def arrived(dst, ri):
        pltpu.make_async_remote_copy(dst, dst, send.at[0], recv.at[ri], device_id=core, device_id_type=MESH).wait_recv()

    lwo = pltpu.make_async_copy(wo_hbm, wo, local.at[0])
    lwi = pltpu.make_async_copy(wi_hbm, wi, local.at[1])
    lwo.start()
    lwi.start()

    partners = [core, zpar, xr, xl, xo, dev(y=ym(y + 1)), dev(y=ym(y - 1))] + [dev(zl=zpeer[o]) for o in zoff]
    barrier = pltpu.get_barrier_semaphore()
    for p in partners:
        pl.semaphore_signal(barrier, inc=1, device_id=p, device_id_type=MESH)

    mine = pl.ds(pl.multiple_of(gx * R, R), R)
    og[mine, :] = og_ref[...]
    inp[mine, :] = in_ref[...]
    pv = pre_ref[...].astype(f32)
    for h in range(2):
        pre_s[h] = pv[:, h * Hh:(h + 1) * Hh]
    pl.semaphore_wait(barrier, len(partners))

    for o in zoff:
        rcopy(og.at[mine, :], og.at[mine, :], S["og_z"] + zl, dev(zl=zpeer[o]))
    rcopy(pre_s.at[oc], pre_r, S["pre_c"], core)
    lwo.wait()
    rcopy(wo.at[pl.ds(pl.multiple_of(oc * Hh, Hh), Hh), :], wo_oth, S["wo"], core)

    def ring_first(view, sl, ss, sc, sgn):
        rcopy(view(y), view(y), sl, dev(y=ym(y + sgn)))
        if LS:
            rcopy(view(y), view(y), ss, dev(y=ym(y - sgn)))
        rcopy(view(y), view(y), sc + y, core)

    def ring_step(view, sl, ss, sc, sgn, s):
        a, b = ym(y - sgn * s), ym(y + sgn * s)
        arrived(view(a), sl + s - 1)
        if s < LL:
            rcopy(view(a), view(a), sl + s, dev(y=ym(y + sgn)))
        rcopy(view(a), view(a), sc + a, core)
        if s <= LS:
            arrived(view(b), ss + s - 1)
            if s < LS:
                rcopy(view(b), view(b), ss + s, dev(y=ym(y - sgn)))
            rcopy(view(b), view(b), sc + b, core)

    def act_view(q):
        return lambda o: acts.at[c, q, o]

    def act_first(i):
        q = zh if i == 0 else 1 - zh
        ring_first(act_view(q), S["act_l"] + i * LL, S["act_s"] + i * LL, S["act_c"] + i * NY, sg * (1 - 2 * i))

    def act_step(i, s):
        q = zh if i == 0 else 1 - zh
        ring_step(act_view(q), S["act_l"] + i * LL, S["act_s"] + i * LL, S["act_c"] + i * NY, sg * (1 - 2 * i), s)

    arrived(pre_r, S["pre_c"])
    own, oth = pre_s[c], pre_r[...]
    first = jnp.where(c == 0, own, oth)
    second = jnp.where(c == 0, oth, own)
    block = jnp.concatenate([first, second], axis=0)
    prez_s[...] = block.astype(bf16)
    rcopy(prez_s, prez_r, S["pre_z"], zpar)
    a, d = activation(block)
    acts[c, zh, y] = a
    slope[zh] = d
    act_first(0)

    def rows(xi, g):
        return pl.ds(pl.multiple_of(xi * XR + g * NZg * R, NZg * R), NZg * R)

    def z_arrived(buf, base, g):
        for t in range(g * NZg, (g + 1) * NZg):
            def go(t=t):
                there = pl.ds(pl.multiple_of((x * NZ + t) * R, R), R)
                arrived(buf.at[there, :], base + t)
            pl.when(zl != t)(go)

    def to_core(xi, g):
        v = rows(xi, g)
        rcopy(og.at[v, :], ogo.at[v, :], S["og_c"] + xi * 2 + g, core)

    def x_first(buf, zbase, xbase, g):
        z_arrived(buf, zbase, g)
        v = buf.at[rows(x, g), :]
        rcopy(v, v, xbase + g, xr)
        rcopy(v, v, xbase + 2 + g, xl)

    left, right, opp = xm(x - 1), xm(x + 1), xm(x + 2)

    def x_left(buf, xbase, g):
        v = buf.at[rows(left, g), :]
        arrived(v, xbase + g)
        if g == 0:
            rcopy(v, v, xbase + 4, xr)

    def x_right(buf, xbase, g):
        v = buf.at[rows(right, g), :]
        arrived(v, xbase + 2 + g)
        if g == 1:
            rcopy(v, v, xbase + 5, xl)

    def x_opp(buf, xbase, g):
        arrived(buf.at[rows(opp, g), :], xbase + 4 + g)

    for g in range(2):
        x_first(og, S["og_z"], S["og_x"], g)
        to_core(x, g)
    act_step(0, 1)
    x_left(og, S["og_x"], 0)
    x_right(og, S["og_x"], 1)
    to_core(left, 0)
    to_core(right, 1)
    x_left(og, S["og_x"], 1)
    to_core(left, 1)
    x_right(og, S["og_x"], 0)
    to_core(right, 0)
    for o in zoff:
        rcopy(inp.at[mine, :], inp.at[mine, :], S["in_z"] + zl, dev(zl=zpeer[o]))

    arrived(prez_r, S["pre_z"])
    a, d = activation(prez_r[...].astype(f32))
    acts[c, 1 - zh, y] = a
    slope[1 - zh] = d
    act_first(1)
    if LL >= 2:
        act_step(0, 2)
    for g in range(2):
        x_opp(og, S["og_x"], g)
        to_core(opp, g)
    arrived(wo_oth, S["wo"])
    for xi in range(NX):
        for g in range(2):
            arrived(ogo.at[rows(xi, g), :], S["og_c"] + xi * 2 + g)

    w_mine = wo.at[pl.ds(pl.multiple_of(c * Hh, Hh), Hh), :]

    def grad_act(dests):
        def lhs(buf):
            return jnp.concatenate(
                [buf[pl.ds(pl.multiple_of((q * NY + d) * B, B), B), :] for d in dests for q in range(2)], axis=0
            )

        v = dot_nt(lhs(og), w_mine[...]) + dot_nt(lhs(ogo), wo_oth[...])
        for i, d in enumerate(dests):
            for q in range(2):
                r0 = (2 * i + q) * B
                for k in range(K):
                    part[k, q, d] = v[r0:r0 + B, k * HC:(k + 1) * HC]

    sk = [sg, -sg]

    def rs_long(k, s):
        d = ym(y + sk[k] * (LL - s + 1))
        v = part[k, :, d]
        if s > 1:
            arrived(rl_r.at[k, s - 2], S["rs_l"] + k * LL + s - 2)
            v = v + rl_r[k, s - 2].astype(f32)
        rl_s[k, s - 1] = v.astype(bf16)
        rcopy(rl_s.at[k, s - 1], rl_r.at[k, s - 1], S["rs_l"] + k * LL + s - 1, dev(y=ym(y + sk[k])))

    def rs_short(k, s):
        d = ym(y - sk[k] * (LS - s + 1))
        v = part[k, :, d]
        if s > 1:
            arrived(rs_r.at[k, s - 2], S["rs_s"] + k * LL + s - 2)
            v = v + rs_r[k, s - 2].astype(f32)
        rs_s[k, s - 1] = v.astype(bf16)
        rcopy(rs_s.at[k, s - 1], rs_r.at[k, s - 1], S["rs_s"] + k * LL + s - 1, dev(y=ym(y - sk[k])))

    grad_act([ym(y + LL)])
    for k in range(K):
        rs_long(k, 1)
    for dist in range(LL - 1, 0, -1):
        grad_act([ym(y + dist), ym(y - dist)])
        if dist == LL - 1:
            for k in range(K):
                rs_short(k, 1)
    grad_act([y])

    for s in range(2, LL + 1):
        for k in range(K):
            rs_long(k, s)
        if s <= LS:
            for k in range(K):
                rs_short(k, s)
        if s == 2:
            for g in range(2):
                x_first(inp, S["in_z"], S["in_x"], g)
            act_step(1, 1)
            if LL >= 3:
                act_step(0, 3)
        if s == 3:
            for g in range(2):
                x_left(inp, S["in_x"], g)
                x_right(inp, S["in_x"], g)
            if LL >= 4:
                act_step(0, 4)
            act_step(1, 2)

    for k in range(K):
        v = part[k, :, y]
        arrived(rl_r.at[k, LL - 1], S["rs_l"] + k * LL + LL - 1)
        v = v + rl_r[k, LL - 1].astype(f32)
        if LS:
            arrived(rs_r.at[k, LS - 1], S["rs_s"] + k * LL + LS - 1)
            v = v + rs_r[k, LS - 1].astype(f32)
        tot[k] = v
        zx_s[k] = v.astype(bf16)
        rcopy(zx_s.at[k], zx_r.at[k], S["zx"] + k, zpar)

    if LL < 3:
        for g in range(2):
            x_left(inp, S["in_x"], g)
            x_right(inp, S["in_x"], g)
        act_step(1, 2)
    for s in range(3, LL + 1):
        act_step(1, s)
    for g in range(2):
        x_opp(inp, S["in_x"], g)

    def gh_view(k):
        return lambda o: gh.at[c, k, :, o]

    for k in range(K):
        arrived(zx_r.at[k], S["zx"] + k)
        v = tot[k] + zx_r[k].astype(f32)
        gh[c, k, :, y] = (v * slope[:, :, k * HC:(k + 1) * HC]).astype(bf16)
        ring_first(gh_view(k), S["gh_l"] + k * LL, S["gh_s"] + k * LL, S["gh_c"] + k * NY, sk[k])

    for i in range(2):
        q = zh if i == 0 else 1 - zh
        for o in range(NY):
            arrived(acts.at[oc, q, o], S["act_c"] + i * NY + o)
    lgo = []

    def grad_w_out(h, k):
        lhs = acts[h].reshape(T, Hh)[:, k * HC:(k + 1) * HC]
        r = slice(h * Hh + k * HC, h * Hh + (k + 1) * HC)
        gwo[r, :] = dot_tn(lhs, og[...]).astype(bf16)
        cp = pltpu.make_async_copy(gwo.at[r, :], gwo_hbm.at[r, :], local.at[2 + h * K + k])
        cp.start()
        lgo.append(cp)

    pieces = [(h, k) for h in range(2) for k in range(K)]

    def grad_in(dests):
        for o in dests:
            for k in range(K):
                arrived(gh.at[oc, k, :, o], S["gh_c"] + k * NY + o)
        v = None
        for h, k in pieces:
            lhs = jnp.concatenate([gh[h, k, :, o].reshape(2 * B, HC) for o in dests], axis=0)
            u = dot_nt(lhs, wi[:, h * Hh + k * HC:h * Hh + (k + 1) * HC])
            v = u if v is None else v + u
        for i, o in enumerate(dests):
            for q in range(2):
                val = v[(2 * i + q) * B:(2 * i + q + 1) * B]
                number = q * NY + o
                owner, j = number // BX, lax.rem(number, BX)
                rel = xm(owner - x)
                xs_s[q, o] = val.astype(bf16)

                def keep(val=val, j=j):
                    xs_own[j] = val

                pl.when(rel == 0)(keep)
                slot = lax.rem(rel + 2, 3)
                rcopy(xs_s.at[q, o], xs_r.at[slot, j], S["xs"] + slot * BX + j, dev(x=owner), when=rel != 0)

    grad_w_out(*pieces[0])
    lwi.wait()
    queue = [[y]] + [[ym(y + s), ym(y - s)] for s in range(1, LL)] + [[ym(y + LL)]]
    for s in range(1, LL + 1):
        for k in range(K):
            ring_step(gh_view(k), S["gh_l"] + k * LL, S["gh_s"] + k * LL, S["gh_c"] + k * NY, sk[k], s)
        grad_in(queue[s - 1])
        if s < len(pieces):
            grad_w_out(*pieces[s])
    grad_in(queue[LL])
    for p in pieces[LL + 1 if LL < len(pieces) else len(pieces):]:
        grad_w_out(*p)

    def grad_w_in(h, k):
        rhs = gh[h, k].reshape(T, HC)
        r = slice(h * Hh + k * HC, h * Hh + (k + 1) * HC)
        gwi[:, r] = dot_tn(inp[...], rhs).astype(bf16)
        cp = pltpu.make_async_copy(gwi.at[:, r], gwi_hbm.at[:, r], local.at[2 + 2 * K + h * K + k])
        cp.start()
        lgo.append(cp)

    for p in pieces[:2]:
        grad_w_in(*p)

    for j in range(BX):
        v = xs_own[j]
        for slot in range(3):
            arrived(xs_r.at[slot, j], S["xs"] + slot * BX + j)
            v = v + xs_r[slot, j].astype(f32)
        z_own[j * B:(j + 1) * B, :] = v
        z_s[j * B:(j + 1) * B, :] = v.astype(bf16)
    for o in reversed(zoff):
        v = z_s.at[pl.ds(pl.multiple_of(zpeer[o] * R, R), R), :]
        rcopy(v, z_r.at[zl], S["zs"] + zl, dev(zl=zpeer[o]))
    for p in pieces[2:]:
        grad_w_in(*p)
    v = z_own[pl.ds(pl.multiple_of(zl * R, R), R), :]
    for o in zoff:
        arrived(z_r.at[zpeer[o]], S["zs"] + zpeer[o])
        v = v + z_r[zpeer[o]].astype(f32)
    gi_ref[...] = v.astype(bf16)

    for cp, when in sends:
        if when is None:
            cp.wait_send()
        else:
            pl.when(when)(cp.wait_send)
    for cp in lgo:
        cp.wait()


def per_device(n_gx, n_gy, inputs, preact, w_in, w_out, out_grad):
    NZ, NY = n_gx // NX, n_gy // 4
    R, W = out_grad.shape
    H = w_out.shape[0]
    Hh, HC = H // 2, H // 2 // K
    T = R * n_gx
    B = T // (2 * NY)
    BX = 2 * NY // NX
    LL = NY // 2
    _, n_recv = layout(NZ, NY)
    V = pltpu.VMEM
    flops = 8 * T * W * H
    return pl.pallas_call(
        functools.partial(kernel, NZ, NY),
        out_shape=(
            jax.ShapeDtypeStruct((R, W), bf16),
            jax.ShapeDtypeStruct((W, H), bf16),
            jax.ShapeDtypeStruct((H, W), bf16),
        ),
        in_specs=[
            pl.BlockSpec(memory_space=V), pl.BlockSpec(memory_space=V),
            pl.BlockSpec(memory_space=pl.ANY), pl.BlockSpec(memory_space=pl.ANY),
            pl.BlockSpec(memory_space=V),
        ],
        out_specs=(
            pl.BlockSpec(memory_space=V), pl.BlockSpec(memory_space=pl.ANY), pl.BlockSpec(memory_space=pl.ANY),
        ),
        scratch_shapes=[
            V((T, W), bf16), V((T, W), bf16), V((T, W), bf16),
            V((W, H), bf16), V((H, W), bf16), V((Hh, W), bf16),
            V((2, B // 2, Hh), f32), V((B // 2, Hh), f32), V((B, Hh), bf16), V((B, Hh), bf16),
            V((2, B, Hh), f32), V((2, 2, NY, B, Hh), bf16), V((K, 2, NY, B, HC), f32),
            V((K, LL, 2, B, HC), bf16), V((K, LL, 2, B, HC), bf16),
            V((K, LL, 2, B, HC), bf16), V((K, LL, 2, B, HC), bf16),
            V((K, 2, B, HC), f32), V((K, 2, B, HC), bf16), V((K, 2, B, HC), bf16),
            V((2, K, 2, NY, B, HC), bf16),
            V((2, NY, B, W), bf16), V((3, BX, B, W), bf16), V((BX, B, W), f32),
            V((R * NZ, W), f32), V((R * NZ, W), bf16), V((NZ, R, W), bf16),
            V((W, H), bf16), V((H, W), bf16),
            pltpu.SemaphoreType.DMA((count_sends(NZ, NY),)),
            pltpu.SemaphoreType.DMA((n_recv,)),
            pltpu.SemaphoreType.DMA((2 + 4 * K,)),
        ],
        compiler_params=pltpu.CompilerParams(
            collective_id=0, has_side_effects=True, vmem_limit_bytes=40 * 1024 * 1024
        ),
        cost_estimate=pl.CostEstimate(flops=flops, bytes_accessed=8 * W * H, transcendentals=2 * B * Hh),
    )(inputs, preact, w_in, w_out, out_grad)


def solution(mesh):
    n_gx, n_gy = mesh.shape["gx"], mesh.shape["gy"]
    placed = (P("gx", "gy"), P("gy", "gx"), P("gy", "gx"), P("gx", "gy"), P("gx", "gy"))
    return jax.shard_map(
        functools.partial(per_device, n_gx, n_gy),
        mesh=mesh,
        in_specs=placed,
        out_specs=(P("gx", "gy"), P("gy", "gx"), P("gx", "gy")),
        check_vma=False,
    )
```

```python
import functools

import jax
import jax.numpy as jnp
from jax import lax
from jax.experimental import pallas as pl
from jax.experimental.pallas import tpu as pltpu
from jax.sharding import PartitionSpec as P

gelu_scale = 0.7978845608028654
cubic_coef = 0.044715
MESH = pl.DeviceIdType.MESH
NX = 4
K = 4
U = 16
bf16, f32 = jnp.bfloat16, jnp.float32


def activation(values):
    argument = gelu_scale * (values + cubic_coef * values * values * values)
    tangent = jnp.tanh(argument)
    acts = (0.5 * values * (1.0 + tangent)).astype(bf16)
    slope = 0.5 * (1.0 + tangent) + 0.5 * values * (1.0 - tangent * tangent) * gelu_scale * (
        1.0 + 3.0 * cubic_coef * values * values
    )
    return acts, slope


def dot_nt(a, b):
    return lax.dot_general(a, b, (((1,), (1,)), ((), ())), preferred_element_type=f32)


def dot_tn(a, b):
    return lax.dot_general(a, b, (((0,), (0,)), ((), ())), preferred_element_type=f32)


class Counter:
    def __init__(self):
        self.n = 0

    def take(self, n=1):
        base = self.n
        self.n += n
        return base


def layout(NZ, NY, rows):
    c, r = Counter(), {}
    for name, n in (
        ("og_z", NZ), ("og_x", 3 * NZ), ("og_c", NX), ("in_z", NZ), ("in_x", 3),
        ("wo", 1), ("pre_c", 1), ("pre_z", 1),
        ("act_l", 2 * (NY // 2)), ("act_s", 2 * (NY // 2)), ("act_c", 2 * NY),
        ("rs_l", K * (NY // 2)), ("rs_s", K * (NY // 2)), ("zx", K),
        ("gh_l", K * (NY // 2)), ("gh_s", K * (NY // 2)), ("gh_c", K * NY),
        ("xs", 3 * (2 * NY // NX)), ("zs", NZ * rows // U),
    ):
        r[name] = c.take(n)
    return r, c.n


def count_sends(NZ, NY):
    return 2 * (NZ - 1) + 3 * NZ + NX + 3 + 3 + 2 * (NY - 1 + NY) + K * (NY - 1) + K + K * (2 * NY - 1) + 2 * NY


def kernel(
    NZ, NY, in_hbm, pre_hbm, wi_hbm, wo_hbm, og_hbm,
    gi_ref, gwi_hbm, gwo_hbm,
    pre_v, og, ogo, inp, wi, wo, wo_oth, pre_s, pre_r, prez_s, prez_r, slope, acts, part,
    rl_s, rl_r, rs_s, rs_r, tot, zx_s, zx_r, gh, xs_s, xs_r, xs_own, z_own, z_s, z_r, gwi, gwo,
    send, recv, local,
):
    R, W = og_hbm.shape
    H = wo_hbm.shape[0]
    Hh, HC = H // 2, H // 2 // K
    T = R * NX * NZ
    XR = R * NZ
    B = T // (2 * NY)
    TB = B // 2
    LL, LS = NY // 2, NY // 2 - 1
    BX = 2 * NY // NX
    S, _ = layout(NZ, NY, R)

    gx, gy = lax.axis_index("gx"), lax.axis_index("gy")
    x, zl = gx // NZ, gx % NZ
    zh, y, c = gy // (2 * NY), (gy // 2) % NY, gy % 2
    oc = 1 - c
    sg = 1 - 2 * c

    def dev(x=x, zl=zl, zh=zh, y=y, c=c):
        return (x * NZ + zl, (zh * NY + y) * 2 + c)

    def ym(v):
        return lax.rem(v + 2 * NY, NY)

    def xm(v):
        return lax.rem(v + 2 * NX, NX)

    core, zpar = dev(c=oc), dev(zh=1 - zh)
    xr, xl, xo = dev(x=xm(x + 1)), dev(x=xm(x - 1)), dev(x=xm(x + 2))
    zoff = range(1, NZ)
    zpeer = {o: lax.rem(zl + o, NZ) for o in zoff}
    near = []
    for i in range(NZ - 1):
        t = 0
        for place in range(NZ):
            order = sorted((p for p in range(NZ) if p != place), key=lambda p: abs(p - place))
            t = jnp.where(zl == place, order[i], t)
        near.append(t)

    sends = []

    def rcopy(src, dst, ri, to, when=None):
        cp = pltpu.make_async_remote_copy(src, dst, send.at[len(sends)], recv.at[ri], device_id=to, device_id_type=MESH)
        sends.append((cp, when))
        if when is None:
            cp.start()
        else:
            pl.when(when)(cp.start)

    def arrived(dst, ri):
        pltpu.make_async_remote_copy(dst, dst, send.at[0], recv.at[ri], device_id=core, device_id_type=MESH).wait_recv()

    partners = [core, zpar, xr, xl, xo, dev(y=ym(y + 1)), dev(y=ym(y - 1))] + [dev(zl=zpeer[o]) for o in zoff]
    barrier = pltpu.get_barrier_semaphore()
    for p in partners:
        pl.semaphore_signal(barrier, inc=1, device_id=p, device_id_type=MESH)

    def piece(xi, t):
        return pl.ds(pl.multiple_of((xi * NZ + t) * R, R), R)

    def column(xi):
        return pl.ds(pl.multiple_of(xi * XR, XR), XR)

    mine = piece(x, zl)
    lpre = pltpu.make_async_copy(pre_hbm, pre_v, local.at[3])
    log = pltpu.make_async_copy(og_hbm, og.at[mine, :], local.at[2])
    lwo = pltpu.make_async_copy(wo_hbm, wo, local.at[0])
    lin = pltpu.make_async_copy(in_hbm, inp.at[mine, :], local.at[4])
    lwi = pltpu.make_async_copy(wi_hbm, wi, local.at[1])
    for cp in (lpre, log, lwo, lin, lwi):
        cp.start()
    pl.semaphore_wait(barrier, len(partners))

    for t in reversed(near):
        rcopy(og_hbm, og.at[mine, :], S["og_z"] + zl, dev(zl=t))

    def x_sends(src, dst, base, step):
        rcopy(src, dst, base, xr)
        rcopy(src, dst, base + step, xl)
        rcopy(src, dst, base + 2 * step, xo)

    x_sends(og_hbm, og.at[mine, :], S["og_x"] + zl, NZ)
    lpre.wait()
    pv = pre_v[...].astype(f32)
    for h in range(2):
        pre_s[h] = pv[:, h * Hh:(h + 1) * Hh]
    rcopy(pre_s.at[oc], pre_r, S["pre_c"], core)
    lwo.wait()
    rcopy(wo.at[pl.ds(pl.multiple_of(oc * Hh, Hh), Hh), :], wo_oth, S["wo"], core)

    def ring_first(view, sl, ss, sc, sgn):
        rcopy(view(y), view(y), sl, dev(y=ym(y + sgn)))
        if LS:
            rcopy(view(y), view(y), ss, dev(y=ym(y - sgn)))
        rcopy(view(y), view(y), sc + y, core)

    def ring_step(view, sl, ss, sc, sgn, s):
        a, b = ym(y - sgn * s), ym(y + sgn * s)
        arrived(view(a), sl + s - 1)
        if s < LL:
            rcopy(view(a), view(a), sl + s, dev(y=ym(y + sgn)))
        rcopy(view(a), view(a), sc + a, core)
        if s <= LS:
            arrived(view(b), ss + s - 1)
            if s < LS:
                rcopy(view(b), view(b), ss + s, dev(y=ym(y - sgn)))
            rcopy(view(b), view(b), sc + b, core)

    def act_view(q):
        return lambda o: acts.at[c, q, o]

    def act_first(i):
        q = zh if i == 0 else 1 - zh
        ring_first(act_view(q), S["act_l"] + i * LL, S["act_s"] + i * LL, S["act_c"] + i * NY, sg * (1 - 2 * i))

    def act_step(i, s):
        if s > LL:
            return
        q = zh if i == 0 else 1 - zh
        ring_step(act_view(q), S["act_l"] + i * LL, S["act_s"] + i * LL, S["act_c"] + i * NY, sg * (1 - 2 * i), s)

    arrived(pre_r, S["pre_c"])
    own, oth = pre_s[c], pre_r[...]
    first = jnp.where(c == 0, own, oth)
    second = jnp.where(c == 0, oth, own)
    block = jnp.concatenate([first, second], axis=0)
    prez_s[...] = block.astype(bf16)
    rcopy(prez_s, prez_r, S["pre_z"], zpar)
    a, d = activation(block)
    acts[c, zh, y] = a
    slope[zh] = d
    act_first(0)

    def to_core(xi):
        v = column(xi)
        rcopy(og.at[v, :], ogo.at[v, :], S["og_c"] + xi, core)

    for t in near:
        v = og.at[piece(x, t), :]
        arrived(v, S["og_z"] + t)
        x_sends(v, v, S["og_x"] + t, NZ)
    log.wait()
    to_core(x)
    act_step(0, 1)
    arrived(prez_r, S["pre_z"])
    a, d = activation(prez_r[...].astype(f32))
    acts[c, 1 - zh, y] = a
    slope[1 - zh] = d
    act_first(1)
    sources = (xm(x - 1), xm(x + 1), xm(x + 2))

    def in_first():
        lin.wait()
        for t in reversed(near):
            rcopy(inp.at[mine, :], inp.at[mine, :], S["in_z"] + zl, dev(zl=t))

    def in_x():
        for t in near:
            arrived(inp.at[piece(x, t), :], S["in_z"] + t)
        v = inp.at[column(x), :]
        x_sends(v, v, S["in_x"], 1)

    def in_last():
        for i, xi in enumerate(sources):
            arrived(inp.at[column(xi), :], S["in_x"] + i)

    for i, xi in enumerate(sources):
        for t in range(NZ):
            arrived(og.at[piece(xi, t), :], S["og_x"] + i * NZ + t)
        to_core(xi)
    in_first()
    act_step(0, 2)
    act_step(1, 1)
    arrived(wo_oth, S["wo"])
    for xi in range(NX):
        arrived(ogo.at[column(xi), :], S["og_c"] + xi)

    w_mine = wo.at[pl.ds(pl.multiple_of(c * Hh, Hh), Hh), :]

    def grad_act(dests):
        def lhs(buf):
            return jnp.concatenate(
                [buf[pl.ds(pl.multiple_of((q * NY + d) * B, B), B), :] for d in dests for q in range(2)], axis=0
            )

        v = dot_nt(lhs(og), w_mine[...]) + dot_nt(lhs(ogo), wo_oth[...])
        for i, d in enumerate(dests):
            for q in range(2):
                r0 = (2 * i + q) * B
                for k in range(K):
                    part[k, q, d] = v[r0:r0 + B, k * HC:(k + 1) * HC]

    sk = [sg if k % 2 == 0 else -sg for k in range(K)]

    def rs_long(k, s):
        d = ym(y + sk[k] * (LL - s + 1))
        v = part[k, :, d]
        if s > 1:
            arrived(rl_r.at[k, s - 2], S["rs_l"] + k * LL + s - 2)
            v = v + rl_r[k, s - 2].astype(f32)
        rl_s[k, s - 1] = v.astype(bf16)
        rcopy(rl_s.at[k, s - 1], rl_r.at[k, s - 1], S["rs_l"] + k * LL + s - 1, dev(y=ym(y + sk[k])))

    def rs_short(k, s):
        d = ym(y - sk[k] * (LS - s + 1))
        v = part[k, :, d]
        if s > 1:
            arrived(rs_r.at[k, s - 2], S["rs_s"] + k * LL + s - 2)
            v = v + rs_r[k, s - 2].astype(f32)
        rs_s[k, s - 1] = v.astype(bf16)
        rcopy(rs_s.at[k, s - 1], rs_r.at[k, s - 1], S["rs_s"] + k * LL + s - 1, dev(y=ym(y - sk[k])))

    grad_act([ym(y + LL)])
    for k in range(K):
        rs_long(k, 1)
    for s in range(1, LL + 1):
        near_y = LL - s
        grad_act([ym(y + near_y), ym(y - near_y)] if near_y else [y])
        if s <= LS:
            for k in range(K):
                rs_short(k, s)
        if s < LL:
            for k in range(K):
                rs_long(k, s + 1)

    for k in range(K):
        v = part[k, :, y]
        arrived(rl_r.at[k, LL - 1], S["rs_l"] + k * LL + LL - 1)
        v = v + rl_r[k, LL - 1].astype(f32)
        if LS:
            arrived(rs_r.at[k, LS - 1], S["rs_s"] + k * LL + LS - 1)
            v = v + rs_r[k, LS - 1].astype(f32)
        tot[k] = v
        zx_s[k] = v.astype(bf16)
        rcopy(zx_s.at[k], zx_r.at[k], S["zx"] + k, zpar)

    in_x()
    for s in range(2, LL):
        act_step(0, s + 1)
        act_step(1, s)

    def gh_view(k):
        return lambda o: gh.at[c, k, :, o]

    for k in range(K):
        arrived(zx_r.at[k], S["zx"] + k)
        v = tot[k] + zx_r[k].astype(f32)
        gh[c, k, :, y] = (v * slope[:, :, k * HC:(k + 1) * HC]).astype(bf16)
        ring_first(gh_view(k), S["gh_l"] + k * LL, S["gh_s"] + k * LL, S["gh_c"] + k * NY, sk[k])

    act_step(1, LL)
    for i in range(2):
        q = zh if i == 0 else 1 - zh
        for o in range(NY):
            arrived(acts.at[oc, q, o], S["act_c"] + i * NY + o)
    lgo = []
    HP = Hh // 2
    pieces = [(h, p) for h in range(2) for p in range(2)]

    def columns(h, p):
        return slice(h * Hh + p * HP, h * Hh + (p + 1) * HP)

    def grad_w_out(h, p):
        r = columns(h, p)
        lhs = acts[h].reshape(T, Hh)[:, p * HP:(p + 1) * HP]
        gwo[r, :] = dot_tn(lhs, og[...]).astype(bf16)
        cp = pltpu.make_async_copy(gwo.at[r, :], gwo_hbm.at[r, :], local.at[5 + h * 2 + p])
        cp.start()
        lgo.append(cp)

    def grad_in(dests):
        for o in dests:
            for k in range(K):
                arrived(gh.at[oc, k, :, o], S["gh_c"] + k * NY + o)
        lhs = jnp.concatenate(
            [
                jnp.concatenate([gh[h, k, :, o].reshape(2 * B, HC) for h in range(2) for k in range(K)], axis=1)
                for o in dests
            ],
            axis=0,
        )
        v = dot_nt(lhs, wi[...])
        for i, o in enumerate(dests):
            for q in range(2):
                val = v[(2 * i + q) * B:(2 * i + q + 1) * B]
                number = q * NY + o
                owner, j = number // BX, lax.rem(number, BX)
                rel = xm(owner - x)
                xs_s[q, o] = val.astype(bf16)

                def keep(val=val, j=j):
                    xs_own[j] = val

                pl.when(rel == 0)(keep)
                slot = lax.rem(rel + 2, 3)
                rcopy(xs_s.at[q, o], xs_r.at[slot, j], S["xs"] + slot * BX + j, dev(x=owner), when=rel != 0)

    def x_sum(dests):
        for o in dests:
            for q in range(2):
                number = q * NY + o
                j = lax.rem(number, BX)

                def go(j=j):
                    v = xs_own[j]
                    for slot in range(3):
                        arrived(xs_r.at[slot, j], S["xs"] + slot * BX + j)
                        v = v + xs_r[slot, j].astype(f32)
                    r = pl.ds(pl.multiple_of(j * B, B), B)
                    z_own[r, :] = v
                    z_s[r, :] = v.astype(bf16)
                    for i in range(B // U):
                        u = j * (B // U) + i
                        to, part_of = u // (R // U), lax.rem(u, R // U)
                        cp = pltpu.make_async_remote_copy(
                            z_s.at[pl.ds(pl.multiple_of(u * U, U), U), :],
                            z_r.at[zl, pl.ds(pl.multiple_of(part_of * U, U), U), :],
                            send.at[count_sends(NZ, NY) + u], recv.at[S["zs"] + zl * (R // U) + part_of],
                            device_id=dev(zl=to), device_id_type=MESH,
                        )
                        pl.when(to != zl)(cp.start)

                pl.when(number // BX == x)(go)

    grad_w_out(*pieces[0])
    lwi.wait()
    queue = [[y]] + [[ym(y + s), ym(y - s)] for s in range(1, LL)] + [[ym(y + LL)]]
    for s in range(1, LL + 1):
        for k in range(K):
            ring_step(gh_view(k), S["gh_l"] + k * LL, S["gh_s"] + k * LL, S["gh_c"] + k * NY, sk[k], s)
        grad_in(queue[s - 1])
        if s < len(pieces):
            grad_w_out(*pieces[s])
        if s >= 2:
            x_sum(queue[s - 2])
    grad_in(queue[LL])
    for p in pieces[LL + 1:]:
        grad_w_out(*p)
    x_sum(queue[LL - 1])

    def grad_w_in(h, p):
        r = columns(h, p)
        n = K // 2
        rhs = jnp.concatenate([gh[h, k].reshape(T, HC) for k in range(p * n, (p + 1) * n)], axis=1)
        gwi[:, r] = dot_tn(inp[...], rhs).astype(bf16)
        cp = pltpu.make_async_copy(gwi.at[:, r], gwi_hbm.at[:, r], local.at[9 + h * 2 + p])
        cp.start()
        lgo.append(cp)

    in_last()
    for p in pieces[:2]:
        grad_w_in(*p)

    x_sum(queue[LL])
    for p in pieces[2:]:
        grad_w_in(*p)
    v = z_own[pl.ds(pl.multiple_of(zl * R, R), R), :]
    for t in near:
        for i in range(R // U):
            arrived(z_r.at[t, i * U:(i + 1) * U, :], S["zs"] + t * (R // U) + i)
        v = v + z_r[t].astype(f32)
    gi_ref[...] = v.astype(bf16)

    for u in range(NZ * R // U):
        row = z_s.at[u * U:(u + 1) * U, :]
        cp = pltpu.make_async_remote_copy(
            row, row, send.at[count_sends(NZ, NY) + u], recv.at[0], device_id=core, device_id_type=MESH
        )
        pl.when(zl != u // (R // U))(cp.wait_send)
    for cp, when in sends:
        if when is None:
            cp.wait_send()
        else:
            pl.when(when)(cp.wait_send)
    for cp in lgo:
        cp.wait()


def per_device(n_gx, n_gy, inputs, preact, w_in, w_out, out_grad):
    NZ, NY = n_gx // NX, n_gy // 4
    R, W = out_grad.shape
    H = w_out.shape[0]
    Hh, HC = H // 2, H // 2 // K
    T = R * n_gx
    B = T // (2 * NY)
    BX = 2 * NY // NX
    LL = NY // 2
    _, n_recv = layout(NZ, NY, R)
    V = pltpu.VMEM
    flops = 8 * T * W * H
    return pl.pallas_call(
        functools.partial(kernel, NZ, NY),
        out_shape=(
            jax.ShapeDtypeStruct((R, W), bf16),
            jax.ShapeDtypeStruct((W, H), bf16),
            jax.ShapeDtypeStruct((H, W), bf16),
        ),
        in_specs=[
            pl.BlockSpec(memory_space=pltpu.HBM),
        ] * 5,
        out_specs=(
            pl.BlockSpec(memory_space=V), pl.BlockSpec(memory_space=pl.ANY), pl.BlockSpec(memory_space=pl.ANY),
        ),
        scratch_shapes=[
            V((B // 2, H), bf16), V((T, W), bf16), V((T, W), bf16), V((T, W), bf16),
            V((W, H), bf16), V((H, W), bf16), V((Hh, W), bf16),
            V((2, B // 2, Hh), f32), V((B // 2, Hh), f32), V((B, Hh), bf16), V((B, Hh), bf16),
            V((2, B, Hh), f32), V((2, 2, NY, B, Hh), bf16), V((K, 2, NY, B, HC), f32),
            V((K, LL, 2, B, HC), bf16), V((K, LL, 2, B, HC), bf16),
            V((K, LL, 2, B, HC), bf16), V((K, LL, 2, B, HC), bf16),
            V((K, 2, B, HC), f32), V((K, 2, B, HC), bf16), V((K, 2, B, HC), bf16),
            V((2, K, 2, NY, B, HC), bf16),
            V((2, NY, B, W), bf16), V((3, BX, B, W), bf16), V((BX, B, W), f32),
            V((R * NZ, W), f32), V((R * NZ, W), bf16), V((NZ, R, W), bf16),
            V((W, H), bf16), V((H, W), bf16),
            pltpu.SemaphoreType.DMA((count_sends(NZ, NY) + NZ * R // U,)),
            pltpu.SemaphoreType.DMA((n_recv,)),
            pltpu.SemaphoreType.DMA((13,)),
        ],
        compiler_params=pltpu.CompilerParams(
            collective_id=0, has_side_effects=True, vmem_limit_bytes=60 * 1024 * 1024
        ),
        cost_estimate=pl.CostEstimate(flops=flops, bytes_accessed=8 * W * H, transcendentals=2 * B * Hh),
    )(inputs, preact, w_in, w_out, out_grad)


def solution(mesh):
    n_gx, n_gy = mesh.shape["gx"], mesh.shape["gy"]
    placed = (P("gx", "gy"), P("gy", "gx"), P("gy", "gx"), P("gx", "gy"), P("gx", "gy"))
    return jax.shard_map(
        functools.partial(per_device, n_gx, n_gy),
        mesh=mesh,
        in_specs=placed,
        out_specs=(P("gx", "gy"), P("gy", "gx"), P("gx", "gy")),
        check_vma=False,
    )
```

```python
import functools

import jax
import jax.numpy as jnp
from jax import lax
from jax.experimental import pallas as pl
from jax.experimental.pallas import tpu as pltpu
from jax.sharding import PartitionSpec as P

gelu_scale = 0.7978845608028654
cubic_coef = 0.044715
MESH = pl.DeviceIdType.MESH
NX = 4
K = 4
U = 16
bf16, f32 = jnp.bfloat16, jnp.float32


def activation(values):
    argument = gelu_scale * (values + cubic_coef * values * values * values)
    tangent = jnp.tanh(argument)
    acts = (0.5 * values * (1.0 + tangent)).astype(bf16)
    slope = 0.5 * (1.0 + tangent) + 0.5 * values * (1.0 - tangent * tangent) * gelu_scale * (
        1.0 + 3.0 * cubic_coef * values * values
    )
    return acts, slope


def dot_nt(a, b):
    return lax.dot_general(a, b, (((1,), (1,)), ((), ())), preferred_element_type=f32)


def dot_tn(a, b):
    return lax.dot_general(a, b, (((0,), (0,)), ((), ())), preferred_element_type=f32)


class Counter:
    def __init__(self):
        self.n = 0

    def take(self, n=1):
        base = self.n
        self.n += n
        return base


def layout(NZ, NY, rows):
    c, r = Counter(), {}
    for name, n in (
        ("og_z", NZ), ("og_x", 3 * NZ), ("og_c", 2 * NX), ("in_z", NZ), ("in_x", 3),
        ("wo", 1), ("pre_c", 1), ("pre_z", 1),
        ("act_l", 2 * (NY // 2)), ("act_s", 2 * (NY // 2)), ("act_c", 2 * NY),
        ("rs_l", K * (NY // 2)), ("rs_s", K * (NY // 2)), ("zx", K),
        ("gh_l", K * (NY // 2)), ("gh_s", K * (NY // 2)), ("gh_c", K * NY),
        ("xs", 3 * (2 * NY // NX)), ("zs", NZ * rows // U),
    ):
        r[name] = c.take(n)
    return r, c.n


def count_sends(NZ, NY):
    return 2 * (NZ - 1) + 3 * NZ + 2 * NX + 3 + 3 + 2 * (NY - 1 + NY) + K * (NY - 1) + K + K * (2 * NY - 1) + 2 * NY


def kernel(
    NZ, NY, in_hbm, pre_hbm, wi_hbm, wo_hbm, og_hbm,
    gi_ref, gwi_hbm, gwo_hbm,
    pre_v, og, ogo, inp, wi, wo, wo_oth, pre_s, pre_r, prez_s, prez_r, slope, acts, part,
    rl_s, rl_r, rs_s, rs_r, tot, zx_s, zx_r, gh, xs_s, xs_r, xs_own, z_own, z_s, z_r, gwi, gwo,
    send, recv, local,
):
    R, W = og_hbm.shape
    H = wo_hbm.shape[0]
    Hh, HC = H // 2, H // 2 // K
    T = R * NX * NZ
    XR = R * NZ
    B = T // (2 * NY)
    TB = B // 2
    LL, LS = NY // 2, NY // 2 - 1
    BX = 2 * NY // NX
    S, _ = layout(NZ, NY, R)

    gx, gy = lax.axis_index("gx"), lax.axis_index("gy")
    x, zl = gx // NZ, gx % NZ
    zh, y, c = gy // (2 * NY), (gy // 2) % NY, gy % 2
    oc = 1 - c
    sg = 1 - 2 * c

    def dev(x=x, zl=zl, zh=zh, y=y, c=c):
        return (x * NZ + zl, (zh * NY + y) * 2 + c)

    def ym(v):
        return lax.rem(v + 2 * NY, NY)

    def xm(v):
        return lax.rem(v + 2 * NX, NX)

    core, zpar = dev(c=oc), dev(zh=1 - zh)
    xr, xl, xo = dev(x=xm(x + 1)), dev(x=xm(x - 1)), dev(x=xm(x + 2))
    zoff = range(1, NZ)
    zpeer = {o: lax.rem(zl + o, NZ) for o in zoff}
    near = []
    for i in range(NZ - 1):
        t = 0
        for place in range(NZ):
            order = sorted((p for p in range(NZ) if p != place), key=lambda p: abs(p - place))
            t = jnp.where(zl == place, order[i], t)
        near.append(t)

    sends = []

    def rcopy(src, dst, ri, to, when=None):
        cp = pltpu.make_async_remote_copy(src, dst, send.at[len(sends)], recv.at[ri], device_id=to, device_id_type=MESH)
        sends.append((cp, when))
        if when is None:
            cp.start()
        else:
            pl.when(when)(cp.start)

    def arrived(dst, ri):
        pltpu.make_async_remote_copy(dst, dst, send.at[0], recv.at[ri], device_id=core, device_id_type=MESH).wait_recv()

    partners = [core, zpar, xr, xl, xo, dev(y=ym(y + 1)), dev(y=ym(y - 1))] + [dev(zl=zpeer[o]) for o in zoff]
    barrier = pltpu.get_barrier_semaphore()
    for p in partners:
        pl.semaphore_signal(barrier, inc=1, device_id=p, device_id_type=MESH)

    def piece(xi, t):
        return pl.ds(pl.multiple_of((xi * NZ + t) * R, R), R)

    def column(xi):
        return pl.ds(pl.multiple_of(xi * XR, XR), XR)

    mine = piece(x, zl)
    lpre = pltpu.make_async_copy(pre_hbm, pre_v, local.at[3])
    log = pltpu.make_async_copy(og_hbm, og.at[mine, :], local.at[2])
    lwo = pltpu.make_async_copy(wo_hbm, wo, local.at[0])
    lin = pltpu.make_async_copy(in_hbm, inp.at[mine, :], local.at[4])
    lwi = pltpu.make_async_copy(wi_hbm, wi, local.at[1])
    for cp in (lpre, log, lwo, lin, lwi):
        cp.start()
    pl.semaphore_wait(barrier, len(partners))

    for t in reversed(near):
        rcopy(og_hbm, og.at[mine, :], S["og_z"] + zl, dev(zl=t))

    def x_sends(src, dst, base, step):
        rcopy(src, dst, base, xr)
        rcopy(src, dst, base + step, xl)
        rcopy(src, dst, base + 2 * step, xo)

    x_sends(og_hbm, og.at[mine, :], S["og_x"] + zl, NZ)
    lpre.wait()
    pv = pre_v[...].astype(f32)
    for h in range(2):
        pre_s[h] = pv[:, h * Hh:(h + 1) * Hh]
    rcopy(pre_s.at[oc], pre_r, S["pre_c"], core)
    lwo.wait()
    rcopy(wo.at[pl.ds(pl.multiple_of(oc * Hh, Hh), Hh), :], wo_oth, S["wo"], core)

    def ring_first(view, sl, ss, sc, sgn):
        rcopy(view(y), view(y), sl, dev(y=ym(y + sgn)))
        if LS:
            rcopy(view(y), view(y), ss, dev(y=ym(y - sgn)))
        rcopy(view(y), view(y), sc + y, core)

    def ring_step(view, sl, ss, sc, sgn, s):
        a, b = ym(y - sgn * s), ym(y + sgn * s)
        arrived(view(a), sl + s - 1)
        if s < LL:
            rcopy(view(a), view(a), sl + s, dev(y=ym(y + sgn)))
        rcopy(view(a), view(a), sc + a, core)
        if s <= LS:
            arrived(view(b), ss + s - 1)
            if s < LS:
                rcopy(view(b), view(b), ss + s, dev(y=ym(y - sgn)))
            rcopy(view(b), view(b), sc + b, core)

    def act_view(q):
        return lambda o: acts.at[c, q, o]

    def act_first(i):
        q = zh if i == 0 else 1 - zh
        ring_first(act_view(q), S["act_l"] + i * LL, S["act_s"] + i * LL, S["act_c"] + i * NY, sg * (1 - 2 * i))

    def act_step(i, s):
        if s > LL:
            return
        q = zh if i == 0 else 1 - zh
        ring_step(act_view(q), S["act_l"] + i * LL, S["act_s"] + i * LL, S["act_c"] + i * NY, sg * (1 - 2 * i), s)

    arrived(pre_r, S["pre_c"])
    own, oth = pre_s[c], pre_r[...]
    first = jnp.where(c == 0, own, oth)
    second = jnp.where(c == 0, oth, own)
    block = jnp.concatenate([first, second], axis=0)
    prez_s[...] = block.astype(bf16)
    rcopy(prez_s, prez_r, S["pre_z"], zpar)
    a, d = activation(block)
    acts[c, zh, y] = a
    slope[zh] = d
    act_first(0)

    def half(xi, g):
        return pl.ds(pl.multiple_of(xi * XR + g * (XR // 2), XR // 2), XR // 2)

    def to_core(xi, g):
        v = half(xi, g)
        rcopy(og.at[v, :], ogo.at[v, :], S["og_c"] + 2 * xi + g, core)

    for t in near:
        v = og.at[piece(x, t), :]
        arrived(v, S["og_z"] + t)
        x_sends(v, v, S["og_x"] + t, NZ)
    log.wait()
    to_core(x, 0)
    to_core(x, 1)
    act_step(0, 1)
    arrived(prez_r, S["pre_z"])
    a, d = activation(prez_r[...].astype(f32))
    acts[c, 1 - zh, y] = a
    slope[1 - zh] = d
    act_first(1)
    sources = (xm(x - 1), xm(x + 1), xm(x + 2))

    def in_first():
        lin.wait()
        for t in reversed(near):
            rcopy(inp.at[mine, :], inp.at[mine, :], S["in_z"] + zl, dev(zl=t))

    def in_x():
        for t in near:
            arrived(inp.at[piece(x, t), :], S["in_z"] + t)
        v = inp.at[column(x), :]
        x_sends(v, v, S["in_x"], 1)

    def in_last():
        for i, xi in enumerate(sources):
            arrived(inp.at[column(xi), :], S["in_x"] + i)

    for i, xi in enumerate(sources):
        for t in range(NZ):
            arrived(og.at[piece(xi, t), :], S["og_x"] + i * NZ + t)
            if (t + 1) % (NZ // 2) == 0:
                to_core(xi, t // (NZ // 2))
    in_first()
    act_step(0, 2)
    act_step(1, 1)
    arrived(wo_oth, S["wo"])
    for xi in range(NX):
        for g in range(2):
            arrived(ogo.at[half(xi, g), :], S["og_c"] + 2 * xi + g)

    w_mine = wo.at[pl.ds(pl.multiple_of(c * Hh, Hh), Hh), :]

    def grad_act(dests):
        def lhs(buf):
            return jnp.concatenate(
                [buf[pl.ds(pl.multiple_of((q * NY + d) * B, B), B), :] for d in dests for q in range(2)], axis=0
            )

        v = dot_nt(lhs(og), w_mine[...]) + dot_nt(lhs(ogo), wo_oth[...])
        for i, d in enumerate(dests):
            for q in range(2):
                r0 = (2 * i + q) * B
                for k in range(K):
                    part[k, q, d] = v[r0:r0 + B, k * HC:(k + 1) * HC]

    sk = [sg if k % 2 == 0 else -sg for k in range(K)]

    def rs_long(k, s):
        d = ym(y + sk[k] * (LL - s + 1))
        v = part[k, :, d]
        if s > 1:
            arrived(rl_r.at[k, s - 2], S["rs_l"] + k * LL + s - 2)
            v = v + rl_r[k, s - 2].astype(f32)
        rl_s[k, s - 1] = v.astype(bf16)
        rcopy(rl_s.at[k, s - 1], rl_r.at[k, s - 1], S["rs_l"] + k * LL + s - 1, dev(y=ym(y + sk[k])))

    def rs_short(k, s):
        d = ym(y - sk[k] * (LS - s + 1))
        v = part[k, :, d]
        if s > 1:
            arrived(rs_r.at[k, s - 2], S["rs_s"] + k * LL + s - 2)
            v = v + rs_r[k, s - 2].astype(f32)
        rs_s[k, s - 1] = v.astype(bf16)
        rcopy(rs_s.at[k, s - 1], rs_r.at[k, s - 1], S["rs_s"] + k * LL + s - 1, dev(y=ym(y - sk[k])))

    grad_act([ym(y + LL)])
    for k in range(K):
        rs_long(k, 1)
    for s in range(1, LL + 1):
        near_y = LL - s
        grad_act([ym(y + near_y), ym(y - near_y)] if near_y else [y])
        if s <= LS:
            for k in range(K):
                rs_short(k, s)
        if s < LL:
            for k in range(K):
                rs_long(k, s + 1)
        if s == 2:
            in_x()

    for k in range(K):
        v = part[k, :, y]
        arrived(rl_r.at[k, LL - 1], S["rs_l"] + k * LL + LL - 1)
        v = v + rl_r[k, LL - 1].astype(f32)
        if LS:
            arrived(rs_r.at[k, LS - 1], S["rs_s"] + k * LL + LS - 1)
            v = v + rs_r[k, LS - 1].astype(f32)
        tot[k] = v
        zx_s[k] = v.astype(bf16)
        rcopy(zx_s.at[k], zx_r.at[k], S["zx"] + k, zpar)

    for s in range(2, LL):
        act_step(0, s + 1)
        act_step(1, s)

    def gh_view(k):
        return lambda o: gh.at[c, k, :, o]

    for k in range(K):
        arrived(zx_r.at[k], S["zx"] + k)
        v = tot[k] + zx_r[k].astype(f32)
        gh[c, k, :, y] = (v * slope[:, :, k * HC:(k + 1) * HC]).astype(bf16)
        ring_first(gh_view(k), S["gh_l"] + k * LL, S["gh_s"] + k * LL, S["gh_c"] + k * NY, sk[k])

    act_step(1, LL)
    for i in range(2):
        q = zh if i == 0 else 1 - zh
        for o in range(NY):
            arrived(acts.at[oc, q, o], S["act_c"] + i * NY + o)
    lgo = []
    HP = Hh // 2
    pieces = [(h, p) for h in range(2) for p in range(2)]

    def columns(h, p):
        return slice(h * Hh + p * HP, h * Hh + (p + 1) * HP)

    def grad_w_out(h, p):
        r = columns(h, p)
        lhs = acts[h].reshape(T, Hh)[:, p * HP:(p + 1) * HP]
        gwo[r, :] = dot_tn(lhs, og[...]).astype(bf16)
        cp = pltpu.make_async_copy(gwo.at[r, :], gwo_hbm.at[r, :], local.at[5 + h * 2 + p])
        cp.start()
        lgo.append(cp)

    def grad_in(dests):
        for o in dests:
            for k in range(K):
                arrived(gh.at[oc, k, :, o], S["gh_c"] + k * NY + o)
        lhs = jnp.concatenate(
            [
                jnp.concatenate([gh[h, k, :, o].reshape(2 * B, HC) for h in range(2) for k in range(K)], axis=1)
                for o in dests
            ],
            axis=0,
        )
        v = dot_nt(lhs, wi[...])
        for i, o in enumerate(dests):
            for q in range(2):
                val = v[(2 * i + q) * B:(2 * i + q + 1) * B]
                number = q * NY + o
                owner, j = number // BX, lax.rem(number, BX)
                rel = xm(owner - x)
                xs_s[q, o] = val.astype(bf16)

                def keep(val=val, j=j):
                    xs_own[j] = val

                pl.when(rel == 0)(keep)
                slot = lax.rem(rel + 2, 3)
                rcopy(xs_s.at[q, o], xs_r.at[slot, j], S["xs"] + slot * BX + j, dev(x=owner), when=rel != 0)

    def x_sum(dests):
        for o in dests:
            for q in range(2):
                number = q * NY + o
                j = lax.rem(number, BX)

                def go(j=j):
                    v = xs_own[j]
                    for slot in range(3):
                        arrived(xs_r.at[slot, j], S["xs"] + slot * BX + j)
                        v = v + xs_r[slot, j].astype(f32)
                    r = pl.ds(pl.multiple_of(j * B, B), B)
                    z_own[r, :] = v
                    z_s[r, :] = v.astype(bf16)
                    for i in range(B // U):
                        u = j * (B // U) + i
                        to, part_of = u // (R // U), lax.rem(u, R // U)
                        cp = pltpu.make_async_remote_copy(
                            z_s.at[pl.ds(pl.multiple_of(u * U, U), U), :],
                            z_r.at[zl, pl.ds(pl.multiple_of(part_of * U, U), U), :],
                            send.at[count_sends(NZ, NY) + u], recv.at[S["zs"] + zl * (R // U) + part_of],
                            device_id=dev(zl=to), device_id_type=MESH,
                        )
                        pl.when(to != zl)(cp.start)

                pl.when(number // BX == x)(go)

    grad_w_out(*pieces[0])
    lwi.wait()
    queue = [[y]] + [[ym(y + s), ym(y - s)] for s in range(1, LL)] + [[ym(y + LL)]]
    for s in range(1, LL + 1):
        for k in range(K):
            ring_step(gh_view(k), S["gh_l"] + k * LL, S["gh_s"] + k * LL, S["gh_c"] + k * NY, sk[k], s)
        grad_in(queue[s - 1])
        if s < len(pieces):
            grad_w_out(*pieces[s])
    grad_in(queue[LL])
    for p in pieces[LL + 1:]:
        grad_w_out(*p)
    for dests in queue[:LL]:
        x_sum(dests)

    def grad_w_in(h, p):
        r = columns(h, p)
        n = K // 2
        rhs = jnp.concatenate([gh[h, k].reshape(T, HC) for k in range(p * n, (p + 1) * n)], axis=1)
        gwi[:, r] = dot_tn(inp[...], rhs).astype(bf16)
        cp = pltpu.make_async_copy(gwi.at[:, r], gwi_hbm.at[:, r], local.at[9 + h * 2 + p])
        cp.start()
        lgo.append(cp)

    in_last()
    for p in pieces[:2]:
        grad_w_in(*p)

    x_sum(queue[LL])
    for p in pieces[2:]:
        grad_w_in(*p)
    v = z_own[pl.ds(pl.multiple_of(zl * R, R), R), :]
    for t in near:
        for i in range(R // U):
            arrived(z_r.at[t, i * U:(i + 1) * U, :], S["zs"] + t * (R // U) + i)
        v = v + z_r[t].astype(f32)
    gi_ref[...] = v.astype(bf16)

    for u in range(NZ * R // U):
        row = z_s.at[u * U:(u + 1) * U, :]
        cp = pltpu.make_async_remote_copy(
            row, row, send.at[count_sends(NZ, NY) + u], recv.at[0], device_id=core, device_id_type=MESH
        )
        pl.when(zl != u // (R // U))(cp.wait_send)
    for cp, when in sends:
        if when is None:
            cp.wait_send()
        else:
            pl.when(when)(cp.wait_send)
    for cp in lgo:
        cp.wait()


def per_device(n_gx, n_gy, inputs, preact, w_in, w_out, out_grad):
    NZ, NY = n_gx // NX, n_gy // 4
    R, W = out_grad.shape
    H = w_out.shape[0]
    Hh, HC = H // 2, H // 2 // K
    T = R * n_gx
    B = T // (2 * NY)
    BX = 2 * NY // NX
    LL = NY // 2
    _, n_recv = layout(NZ, NY, R)
    V = pltpu.VMEM
    flops = 8 * T * W * H
    return pl.pallas_call(
        functools.partial(kernel, NZ, NY),
        out_shape=(
            jax.ShapeDtypeStruct((R, W), bf16),
            jax.ShapeDtypeStruct((W, H), bf16),
            jax.ShapeDtypeStruct((H, W), bf16),
        ),
        in_specs=[
            pl.BlockSpec(memory_space=pltpu.HBM),
        ] * 5,
        out_specs=(
            pl.BlockSpec(memory_space=V), pl.BlockSpec(memory_space=pl.ANY), pl.BlockSpec(memory_space=pl.ANY),
        ),
        scratch_shapes=[
            V((B // 2, H), bf16), V((T, W), bf16), V((T, W), bf16), V((T, W), bf16),
            V((W, H), bf16), V((H, W), bf16), V((Hh, W), bf16),
            V((2, B // 2, Hh), f32), V((B // 2, Hh), f32), V((B, Hh), bf16), V((B, Hh), bf16),
            V((2, B, Hh), f32), V((2, 2, NY, B, Hh), bf16), V((K, 2, NY, B, HC), f32),
            V((K, LL, 2, B, HC), bf16), V((K, LL, 2, B, HC), bf16),
            V((K, LL, 2, B, HC), bf16), V((K, LL, 2, B, HC), bf16),
            V((K, 2, B, HC), f32), V((K, 2, B, HC), bf16), V((K, 2, B, HC), bf16),
            V((2, K, 2, NY, B, HC), bf16),
            V((2, NY, B, W), bf16), V((3, BX, B, W), bf16), V((BX, B, W), f32),
            V((R * NZ, W), f32), V((R * NZ, W), bf16), V((NZ, R, W), bf16),
            V((W, H), bf16), V((H, W), bf16),
            pltpu.SemaphoreType.DMA((count_sends(NZ, NY) + NZ * R // U,)),
            pltpu.SemaphoreType.DMA((n_recv,)),
            pltpu.SemaphoreType.DMA((13,)),
        ],
        compiler_params=pltpu.CompilerParams(
            collective_id=0, has_side_effects=True, vmem_limit_bytes=60 * 1024 * 1024
        ),
        cost_estimate=pl.CostEstimate(flops=flops, bytes_accessed=8 * W * H, transcendentals=2 * B * Hh),
    )(inputs, preact, w_in, w_out, out_grad)


def solution(mesh):
    n_gx, n_gy = mesh.shape["gx"], mesh.shape["gy"]
    placed = (P("gx", "gy"), P("gy", "gx"), P("gy", "gx"), P("gx", "gy"), P("gx", "gy"))
    return jax.shard_map(
        functools.partial(per_device, n_gx, n_gy),
        mesh=mesh,
        in_specs=placed,
        out_specs=(P("gx", "gy"), P("gy", "gx"), P("gx", "gy")),
        check_vma=False,
    )
```
